512 devices in a mesh: pipe: 4 (over y_lo), dp: 16 (over x, y_hi, core), tensor: 8 (over z).
Axes of the slice: x: 4, y: 8 (y_hi: 2, y_lo: 4; y = y_hi * 4 + y_lo), z: 8, core: 2. Of those that a mesh axis runs over, the one named last changes fastest.
Arguments:
- saved: bfloat16 [4, 4, 96, 4096], P('pipe', None, 'dp', 'tensor'), may hold values from -6 to 6
- pool: bfloat16 [8, 96, 4096], P(None, 'dp', 'tensor'), may hold values from -6 to 6
- picked: int32 [4], replicated, may hold values from 0 to 7
- w_up: bfloat16 [4, 4096, 14336], P('pipe', 'tensor', 'dp'), may hold values from -0.09375 to 0.09375
- w_down: bfloat16 [4, 14336, 4096], P('pipe', 'dp', 'tensor'), may hold values from -0.046875 to 0.046875
Outputs:
- input_grads: bfloat16 [4, 4, 96, 4096], P('pipe', None, 'dp', 'tensor')
- grad_up: bfloat16 [4, 4096, 14336], P('pipe', 'tensor', 'dp')
- grad_down: bfloat16 [4, 14336, 4096], P('pipe', 'dp', 'tensor')
The draws below stay inside these ranges and needn't reach their ends.
All inputs are finite; a program needn't handle non-finite values.
Results may differ from the reference program's by a relative error of at most 0.034.
Values may be sent and summed in bfloat16 or wider, within the bound.
No kernel may reach another device: no remote copies, remote signals or barrier semaphores. Data moves between devices by JAX's collectives and lax.ppermute only.
A program may use at most 128 MiB of HBM per device.

```python
import jax
import jax.numpy as jnp
from jax import lax

D = 4096
FF = 14336
MB = 4
POOL = 8
SEGMENTS = 4
TOK = 96
N_TENSOR = 8


def plant(array, key, smallest, top_value):
    longest = array.shape.index(max(array.shape))
    spots = []
    for shift in (0, 1):
        where = [jax.random.randint(jax.random.fold_in(key, axis), (), 0, length) for axis, length in enumerate(array.shape)]
        where[longest] = (where[longest] + shift) % array.shape[longest]
        spots.append(tuple(where))
    return array.at[spots[0]].set(smallest).at[spots[1]].set(top_value)


def levels(stream_key, extent, shards, smallest, high):
    def one(dim, blocks):
        draws = jax.random.uniform(jax.random.fold_in(jax.random.fold_in(stream_key, 6), dim), (blocks,), jnp.float32, smallest / len(shards), high / len(shards))
        return jnp.repeat(jnp.exp(draws), extent[dim] // blocks).reshape((-1,) + (1,) * (len(extent) - dim - 1))

    level = one(*shards[0])
    for cut in shards[1:]:
        level = level * one(*cut)
    return level


def bell_draw(own_key, dims, width, most, shards=(), dtype=jnp.bfloat16):
    array = width * jax.random.normal(own_key, dims, jnp.float32)
    if shards:
        array = array * levels(own_key, dims, shards, -0.22, 0.18)
    return jnp.clip(array, -most, most).astype(dtype)


def setup_inputs(seed: int = 0) -> dict:
    splits = jax.random.split(jax.random.key(seed), 6)
    saved = bell_draw(splits[0], (SEGMENTS, MB, TOK, D), 1.0, 6.0, ((0, 4), (2, 16), (3, 8)))
    pool = bell_draw(splits[1], (POOL, TOK, D), 1.0, 6.0, ((1, 16), (2, 8)))
    picked = plant(jax.random.randint(splits[2], (MB,), 0, POOL), jax.random.fold_in(splits[2], 1), 0, POOL - 1).astype(jnp.int32)
    w_up = bell_draw(splits[3], (SEGMENTS, D, FF), D ** -0.5, 0.09375, ((0, 4), (1, 8), (2, 16)))
    w_down = bell_draw(splits[4], (SEGMENTS, FF, D), FF ** -0.5, 0.046875, ((0, 4), (1, 16), (2, 8)))
    return {"saved": saved, "pool": pool, "picked": picked, "w_up": w_up, "w_down": w_down}


def block_sum(left, right):
    tokens = left.shape[0]
    pieces = jnp.einsum("tkd,kdf->ktf", left.reshape(tokens, N_TENSOR, -1).astype(jnp.float32), right.astype(jnp.float32))
    rounded = lax.optimization_barrier(pieces.astype(jnp.bfloat16))
    return jnp.sum(rounded.astype(jnp.float32), axis=0)


def reference(saved, pool, picked, w_up, w_down):
    incoming = [pool[picked[m]] for m in range(MB)]
    grads_list = [None] * SEGMENTS
    up_list = [None] * SEGMENTS
    down_list = [None] * SEGMENTS
    for segment in reversed(range(SEGMENTS)):
        up_w = w_up[segment]
        down_w = w_down[segment]
        up_blocks = up_w.reshape(N_TENSOR, D // N_TENSOR, FF)
        down_blocks = jnp.transpose(down_w.reshape(FF, N_TENSOR, D // N_TENSOR), (1, 2, 0))
        outgoing, hiddens, up_grads = [], [], []
        for m in range(MB):
            inputs = saved[segment, m]
            arriving = incoming[m]
            up = block_sum(inputs, up_blocks)
            back = block_sum(arriving, down_blocks)
            sig = jax.nn.sigmoid(up)
            hidden = (up * sig).astype(jnp.bfloat16)
            d_up = (back * sig * (1.0 + up * (1.0 - sig))).astype(jnp.bfloat16)
            mixed = jnp.dot(d_up, up_w.T, preferred_element_type=jnp.float32)
            outgoing.append((arriving.astype(jnp.float32) + mixed).astype(jnp.bfloat16))
            hiddens.append(hidden)
            up_grads.append(d_up)
        all_inputs = saved[segment].reshape(MB * TOK, D)
        all_arriving = jnp.stack(incoming).reshape(MB * TOK, D)
        up_list[segment] = jnp.dot(all_inputs.T, jnp.stack(up_grads).reshape(MB * TOK, FF), preferred_element_type=jnp.float32).astype(jnp.bfloat16)
        down_list[segment] = jnp.dot(jnp.stack(hiddens).reshape(MB * TOK, FF).T, all_arriving, preferred_element_type=jnp.float32).astype(jnp.bfloat16)
        grads_list[segment] = jnp.stack(outgoing)
        incoming = outgoing
    return jnp.stack(grads_list), jnp.stack(up_list), jnp.stack(down_list)
```

```python
import jax
import jax.numpy as jnp
from jax import lax
from jax.sharding import PartitionSpec as P

GROUPS = 1
BF16 = jnp.bfloat16
F32 = jnp.float32


def swap_cores(x):
    peers = lax.axis_size("dp")
    return lax.ppermute(x, "dp", [(i, i ^ 1) for i in range(peers)])


def chips_exchange(x):
    peers = lax.axis_size("dp")
    groups = [[i for i in range(peers) if i % 2 == core] for core in range(2)]
    return lax.all_to_all(x, "dp", 0, 0, axis_index_groups=groups, tiled=True)


def features_exchange(x):
    return lax.all_to_all(x, "tensor", 0, 0, tiled=True)


def copies(x, count):
    return jnp.broadcast_to(x[None], (count,) + x.shape)


def add_blocks(x):
    return jnp.sum(x.astype(F32), axis=0)


def by_cols(left, right):
    return lax.dot_general(
        left, right, (((left.ndim - 1,), (1,)), ((), ())), preferred_element_type=F32
    ).astype(BF16)


def by_rows(left, right):
    dims = tuple(range(left.ndim - 1))
    return lax.dot_general(left, right, ((dims, dims), ((), ())), preferred_element_type=F32)


def body(saved, pool, picked, w_up, w_down):
    segments = lax.axis_size("pipe")
    segment = lax.axis_index("pipe")
    chips = lax.axis_size("dp") // 2
    parts = lax.axis_size("tensor")
    micro_count, rows, width = saved.shape[1:]
    units = w_up.shape[2]
    size = micro_count // GROUPS
    block = size * rows

    up_w = jnp.concatenate([w_up[0], swap_cores(w_up[0])], axis=1)
    down_w = jnp.concatenate([w_down[0], swap_cores(w_down[0])], axis=0)

    full_in = chips_exchange(copies(saved[0].reshape(micro_count * rows, width), chips))
    up_part = lax.dot_general(
        full_in, up_w, (((2,), (0,)), ((), ())), preferred_element_type=F32
    ).astype(BF16)
    up = add_blocks(features_exchange(up_part))
    sig = jax.nn.sigmoid(up)
    hidden = (up * sig).astype(BF16)
    slope = (sig * (1.0 + up * (1.0 - sig))).reshape(GROUPS, block, 2 * units)

    fresh = jnp.stack(
        [lax.dynamic_index_in_dim(pool, picked[m], 0, keepdims=False) for m in range(micro_count)]
    ).reshape(GROUPS, block, width)

    pad = segments - 1
    slots = GROUPS + 2 * pad
    all_in = full_in.reshape(chips, GROUPS, block, width)
    kept_out = jnp.zeros((slots, block, width), BF16)
    kept_back = jnp.zeros((slots, chips, block, width), BF16)
    kept_d_up = jnp.zeros((slots, chips, block, 2 * units), BF16)
    carried = jnp.zeros((block, width), BF16)
    for tick in range(GROUPS + pad):
        group = tick - (pad - segment)
        slot = jnp.clip(group, 0, GROUPS - 1)
        last = lax.dynamic_index_in_dim(fresh, slot, 0, keepdims=False)
        if tick == 0:
            arriving = last
        else:
            pairs = [(i, i - 1) for i in range(1, segments)]
            received = lax.ppermute(carried, "pipe", pairs)
            arriving = jnp.where(segment == segments - 1, last, received)
        full_back = chips_exchange(copies(arriving, chips))
        back = add_blocks(features_exchange(by_cols(full_back, down_w)))
        here = lax.dynamic_index_in_dim(slope, slot, 0, keepdims=False)
        d_up = (back * here).astype(BF16)
        full_d_up = features_exchange(copies(d_up, parts))
        mixed = add_blocks(chips_exchange(by_cols(full_d_up, up_w)))
        carried = (arriving.astype(F32) + mixed).astype(BF16)
        kept_out = lax.dynamic_update_index_in_dim(kept_out, carried, group + pad, 0)
        kept_back = lax.dynamic_update_index_in_dim(kept_back, full_back, group + pad, 0)
        kept_d_up = lax.dynamic_update_index_in_dim(kept_d_up, full_d_up, group + pad, 0)

    grads_in = kept_out[pad : pad + GROUPS].reshape(micro_count, rows, width)
    all_back = kept_back[pad : pad + GROUPS]
    all_d_up = kept_d_up[pad : pad + GROUPS]
    full_hidden = features_exchange(copies(hidden, parts)).reshape(chips, GROUPS, block, 2 * units)
    all_in = jnp.swapaxes(all_in, 0, 1)
    full_hidden = jnp.swapaxes(full_hidden, 0, 1)

    grad_up = by_rows(all_in, all_d_up[..., :units]) + by_rows(
        swap_cores(all_in), swap_cores(all_d_up[..., units:])
    )
    grad_down = by_rows(full_hidden[..., :units], all_back) + by_rows(
        swap_cores(full_hidden[..., units:]), swap_cores(all_back)
    )
    return (grads_in[None], grad_up.astype(BF16)[None], grad_down.astype(BF16)[None])


def solution(mesh):
    return jax.shard_map(
        body,
        mesh=mesh,
        in_specs=(
            P("pipe", None, "dp", "tensor"),
            P(None, "dp", "tensor"),
            P(),
            P("pipe", "tensor", "dp"),
            P("pipe", "dp", "tensor"),
        ),
        out_specs=(
            P("pipe", None, "dp", "tensor"),
            P("pipe", "tensor", "dp"),
            P("pipe", "dp", "tensor"),
        ),
        check_vma=False,
    )
```

```python
import jax
import jax.numpy as jnp
from jax import lax
from jax.sharding import PartitionSpec as P

BF16 = jnp.bfloat16
F32 = jnp.float32


def swap_cores(x):
    peers = lax.axis_size("dp")
    return lax.ppermute(x, "dp", [(i, i ^ 1) for i in range(peers)])


def chips_exchange(x):
    peers = lax.axis_size("dp")
    groups = [[i for i in range(peers) if i % 2 == core] for core in range(2)]
    return lax.all_to_all(x, "dp", 0, 0, axis_index_groups=groups, tiled=True)


def features_exchange(x):
    return lax.all_to_all(x, "tensor", 0, 0, tiled=True)


def copies(x, count):
    return jnp.broadcast_to(x[None], (count,) + x.shape)


def add_blocks(x):
    return jnp.sum(x.astype(F32), axis=0)


def by_cols(left, right):
    return lax.dot_general(
        left, right, (((left.ndim - 1,), (1,)), ((), ())), preferred_element_type=F32
    ).astype(BF16)


def by_rows(left, right):
    dims = tuple(range(left.ndim - 1))
    return lax.dot_general(left, right, ((dims, dims), ((), ())), preferred_element_type=F32)


def body(saved, pool, picked, w_up, w_down):
    segments = lax.axis_size("pipe")
    segment = lax.axis_index("pipe")
    chips = lax.axis_size("dp") // 2
    parts = lax.axis_size("tensor")
    micro_count, rows, width = saved.shape[1:]
    units = w_up.shape[2]
    block = micro_count * rows
    last = segments - 1

    up_w = jnp.concatenate([w_up[0], swap_cores(w_up[0])], axis=1)
    down_w = jnp.concatenate([w_down[0], swap_cores(w_down[0])], axis=0)

    fresh = jnp.zeros((micro_count, rows, width), BF16)
    for sample in range(pool.shape[0]):
        fresh = jnp.where((picked == sample)[:, None, None], pool[sample][None], fresh)
    fresh = fresh.reshape(block, width)

    gathered = chips_exchange(
        copies(jnp.concatenate([saved[0].reshape(block, width), fresh], axis=0), chips)
    )
    full_in = gathered[:, :block]
    full_back = gathered[:, block:]
    up_part = lax.dot_general(
        full_in, up_w, (((2,), (0,)), ((), ())), preferred_element_type=F32
    ).astype(BF16)
    back_part = by_cols(full_back, down_w)
    sums = add_blocks(features_exchange(jnp.concatenate([up_part, back_part], axis=1)))
    up = sums[:block]
    sig = jax.nn.sigmoid(up)
    hidden = (up * sig).astype(BF16)
    slope = sig * (1.0 + up * (1.0 - sig))

    def second_half(arriving, back):
        d_up = (back * slope).astype(BF16)
        full_d_up = features_exchange(copies(d_up, parts))
        mixed = add_blocks(chips_exchange(by_cols(full_d_up, up_w)))
        return (arriving.astype(F32) + mixed).astype(BF16), full_d_up

    def gather_hidden():
        return features_exchange(copies(hidden, parts))

    def tick(arriving):
        full_back = chips_exchange(copies(arriving, chips))
        back = add_blocks(features_exchange(by_cols(full_back, down_w)))
        out, full_d_up = second_half(arriving, back)
        return out, full_back, full_d_up

    def first_tick():
        out, full_d_up = second_half(fresh, sums[block:])
        return out, full_d_up, jnp.zeros((parts, block, 2 * units), BF16)

    def wait_first():
        return (
            jnp.zeros((block, width), BF16),
            jnp.zeros((parts, block, 2 * units), BF16),
            gather_hidden(),
        )

    out, full_d_up, full_hidden = lax.cond(segment == last, first_tick, wait_first)
    for at in range(last - 1, -1, -1):
        received = lax.ppermute(out, "pipe", [(at + 1, at)])
        out, full_back, full_d_up = lax.cond(
            segment == at,
            lambda received, out, full_back, full_d_up: tick(received),
            lambda received, out, full_back, full_d_up: (out, full_back, full_d_up),
            received,
            out,
            full_back,
            full_d_up,
        )
    full_hidden = lax.cond(segment == last, gather_hidden, lambda: full_hidden)

    grad_up = by_rows(full_in, full_d_up[..., :units]) + by_rows(
        swap_cores(full_in), swap_cores(full_d_up[..., units:])
    )
    grad_down = by_rows(full_hidden[..., :units], full_back) + by_rows(
        swap_cores(full_hidden[..., units:]), swap_cores(full_back)
    )
    grads_in = out.reshape(micro_count, rows, width)
    return (grads_in[None], grad_up.astype(BF16)[None], grad_down.astype(BF16)[None])


def solution(mesh):
    return jax.shard_map(
        body,
        mesh=mesh,
        in_specs=(
            P("pipe", None, "dp", "tensor"),
            P(None, "dp", "tensor"),
            P(),
            P("pipe", "tensor", "dp"),
            P("pipe", "dp", "tensor"),
        ),
        out_specs=(
            P("pipe", None, "dp", "tensor"),
            P("pipe", "tensor", "dp"),
            P("pipe", "dp", "tensor"),
        ),
        check_vma=False,
    )
```

```python
import jax
import jax.numpy as jnp
from jax import lax
from jax.sharding import PartitionSpec as P

BF16 = jnp.bfloat16
F32 = jnp.float32


def swap_cores(x):
    peers = lax.axis_size("dp")
    return lax.ppermute(x, "dp", [(i, i ^ 1) for i in range(peers)])


def chips_exchange(x):
    peers = lax.axis_size("dp")
    groups = [[i for i in range(peers) if i % 2 == core] for core in range(2)]
    return lax.all_to_all(x, "dp", 0, 0, axis_index_groups=groups, tiled=True)


def features_exchange(x):
    return lax.all_to_all(x, "tensor", 0, 0, tiled=True)


def copies(x, count):
    return jnp.broadcast_to(x[None], (count,) + x.shape)


def add_blocks(x):
    return jnp.sum(x.astype(F32), axis=0)


def by_cols(left, right):
    return lax.dot_general(
        left, right, (((left.ndim - 1,), (1,)), ((), ())), preferred_element_type=F32
    ).astype(BF16)


def by_rows(left, right):
    dims = tuple(range(left.ndim - 1))
    return lax.dot_general(left, right, ((dims, dims), ((), ())), preferred_element_type=F32)


def body(saved, pool, picked, w_up, w_down):
    segments = lax.axis_size("pipe")
    segment = lax.axis_index("pipe")
    chips = lax.axis_size("dp") // 2
    parts = lax.axis_size("tensor")
    micro_count, rows, width = saved.shape[1:]
    units = w_up.shape[2]
    block = micro_count * rows
    last = segments - 1

    up_w = jnp.concatenate([w_up[0], swap_cores(w_up[0])], axis=1)
    down_w = jnp.concatenate([w_down[0], swap_cores(w_down[0])], axis=0)

    samples = jnp.swapaxes(pool, 0, 1)
    fresh = jnp.zeros((rows, micro_count, width), BF16)
    for sample in range(pool.shape[0]):
        fresh = jnp.where((picked == sample)[None, :, None], samples[:, sample][:, None], fresh)
    fresh = fresh.reshape(block, width)
    inputs = jnp.swapaxes(saved[0], 0, 1).reshape(block, width)

    gathered = chips_exchange(copies(jnp.concatenate([inputs, fresh], axis=0), chips))
    full_in = gathered[:, :block]
    full_back = gathered[:, block:]
    up_part = lax.dot_general(
        full_in, up_w, (((2,), (0,)), ((), ())), preferred_element_type=F32
    ).astype(BF16)
    back_part = by_cols(full_back, down_w)
    sums = add_blocks(features_exchange(jnp.concatenate([up_part, back_part], axis=1)))
    up = sums[:block]
    sig = jax.nn.sigmoid(up)
    hidden = (up * sig).astype(BF16)
    slope = sig * (1.0 + up * (1.0 - sig))

    def second_half(arriving, back):
        d_up = (back * slope).astype(BF16)
        full_d_up = features_exchange(copies(d_up, parts))
        mixed = add_blocks(chips_exchange(by_cols(full_d_up, up_w)))
        return (arriving.astype(F32) + mixed).astype(BF16), full_d_up

    def both_cores(x):
        return jnp.concatenate([x, swap_cores(x)], axis=0)

    def own_units(x):
        return jnp.concatenate([x[..., :units], swap_cores(x[..., units:])], axis=0)

    def own_hidden():
        return own_units(features_exchange(copies(hidden, parts)))

    def weight_grads(all_in, all_hidden, full_back, full_d_up):
        grad_up = by_rows(all_in, own_units(full_d_up)).astype(BF16)
        grad_down = by_rows(all_hidden, both_cores(full_back)).astype(BF16)
        return grad_up, grad_down

    def tick(arriving):
        full_back = chips_exchange(copies(arriving, chips))
        back = add_blocks(features_exchange(by_cols(full_back, down_w)))
        out, full_d_up = second_half(arriving, back)
        return out, full_back, full_d_up

    def first_tick():
        out, full_d_up = second_half(fresh, sums[block:])
        return (
            out,
            full_d_up,
            jnp.zeros((2 * chips, block, width), BF16),
            jnp.zeros((2 * parts, block, units), BF16),
        )

    def wait_first():
        return (
            jnp.zeros((block, width), BF16),
            jnp.zeros((parts, block, 2 * units), BF16),
            both_cores(full_in),
            own_hidden(),
        )

    out, full_d_up, all_in, all_hidden = lax.cond(segment == last, first_tick, wait_first)
    for at in range(last - 1, 0, -1):
        received = lax.ppermute(out, "pipe", [(at + 1, at)])
        out, full_back, full_d_up = lax.cond(
            segment == at,
            lambda received, out, full_back, full_d_up: tick(received),
            lambda received, out, full_back, full_d_up: (out, full_back, full_d_up),
            received,
            out,
            full_back,
            full_d_up,
        )
    received = lax.ppermute(out, "pipe", [(1, 0)])

    def end_lowest():
        out, full_back, full_d_up = tick(received)
        return (out,) + weight_grads(all_in, all_hidden, full_back, full_d_up)

    def end_middle():
        return (out,) + weight_grads(all_in, all_hidden, full_back, full_d_up)

    def end_highest():
        return (out,) + weight_grads(both_cores(full_in), own_hidden(), full_back, full_d_up)

    which = jnp.where(segment == 0, 0, jnp.where(segment == last, 2, 1))
    out, grad_up, grad_down = lax.switch(which, (end_lowest, end_middle, end_highest))
    grads_in = jnp.swapaxes(out.reshape(rows, micro_count, width), 0, 1)
    return grads_in[None], grad_up[None], grad_down[None]


def solution(mesh):
    return jax.shard_map(
        body,
        mesh=mesh,
        in_specs=(
            P("pipe", None, "dp", "tensor"),
            P(None, "dp", "tensor"),
            P(),
            P("pipe", "tensor", "dp"),
            P("pipe", "dp", "tensor"),
        ),
        out_specs=(
            P("pipe", None, "dp", "tensor"),
            P("pipe", "tensor", "dp"),
            P("pipe", "dp", "tensor"),
        ),
        check_vma=False,
    )
```

```python
import jax
import jax.numpy as jnp
from jax import lax
from jax.sharding import PartitionSpec as P

BF16 = jnp.bfloat16
F32 = jnp.float32


def swap_cores(x):
    peers = lax.axis_size("dp")
    return lax.ppermute(x, "dp", [(i, i ^ 1) for i in range(peers)])


def chips_exchange(x):
    peers = lax.axis_size("dp")
    groups = [[i for i in range(peers) if i % 2 == core] for core in range(2)]
    return lax.all_to_all(x, "dp", 0, 0, axis_index_groups=groups, tiled=True)


def row_exchange(x):
    peers = lax.axis_size("dp")
    groups = [[4 * at + r for at in range(peers // 4)] for r in range(4)]
    return lax.all_to_all(x, "dp", 0, 0, axis_index_groups=groups, tiled=True)


def swap_middle(x, mate):
    segments, peers = lax.axis_size("pipe"), lax.axis_size("dp")
    pairs = [(p * peers + i, p * peers + (i ^ mate)) for p in range(1, segments - 1) for i in range(peers)]
    return lax.ppermute(x, ("pipe", "dp"), pairs)


def swap_mates(x, mate):
    return lax.ppermute(x, "dp", [(i, i ^ mate) for i in range(lax.axis_size("dp"))])


def features_exchange(x):
    return lax.all_to_all(x, "tensor", 0, 0, tiled=True)


def copies(x, count):
    return jnp.broadcast_to(x[None], (count,) + x.shape)


def add_blocks(x):
    return jnp.sum(x.astype(F32), axis=0)


def cols_product(left, right):
    return lax.dot_general(
        left, right, (((left.ndim - 1,), (1,)), ((), ())), preferred_element_type=F32
    )


def by_cols(left, right):
    return cols_product(left, right).astype(BF16)


def by_rows(left, right):
    dims = tuple(range(left.ndim - 1))
    return lax.dot_general(left, right, ((dims, dims), ((), ())), preferred_element_type=F32)


def body(saved, pool, picked, w_up, w_down):
    segments = lax.axis_size("pipe")
    segment = lax.axis_index("pipe")
    chips = lax.axis_size("dp") // 2
    parts = lax.axis_size("tensor")
    micro_count, rows, width = saved.shape[1:]
    units = w_up.shape[2]
    block = micro_count * rows
    last = segments - 1
    peers = lax.axis_size("dp")
    few = chips // 2
    y_hi = (lax.axis_index("dp") // 2) % 2

    up_w = jnp.concatenate([w_up[0], swap_cores(w_up[0])], axis=1)
    down_w = jnp.concatenate([w_down[0], swap_cores(w_down[0])], axis=0)

    up_other = swap_middle(w_up[0], 2)
    down_other = swap_middle(w_down[0], 2)

    samples = jnp.swapaxes(pool, 0, 1)
    fresh = jnp.zeros((rows, micro_count, width), BF16)
    for sample in range(pool.shape[0]):
        fresh = jnp.where((picked == sample)[None, :, None], samples[:, sample][:, None], fresh)
    fresh = fresh.reshape(block, width)
    inputs = jnp.swapaxes(saved[0], 0, 1).reshape(block, width)

    gathered = chips_exchange(copies(jnp.concatenate([inputs, fresh], axis=0), chips))
    full_in = gathered[:, :block]
    full_back = gathered[:, block:]
    up_part = lax.dot_general(
        full_in, up_w, (((2,), (0,)), ((), ())), preferred_element_type=F32
    ).astype(BF16)
    back_part = by_cols(full_back, down_w)
    sums = add_blocks(features_exchange(jnp.concatenate([up_part, back_part], axis=1)))
    up = sums[:block]
    sig = jax.nn.sigmoid(up)
    hidden = (up * sig).astype(BF16)
    slope = sig * (1.0 + up * (1.0 - sig))

    moves = []
    for group in range(1, last):
        for i in range(peers):
            for z in range(parts):
                units_y, tokens_y = (i // 2) % 2, z % 2
                to = i - 2 * units_y + 2 * tokens_y
                place = (units_y ^ tokens_y) * few + z // 2
                moves.append(((group * peers + i) * parts + z, (group * peers + to) * parts + place))

    def middle_weights():
        return (
            jnp.concatenate([up_other, swap_middle(up_other, 1)], axis=1),
            jnp.concatenate([down_other, swap_middle(down_other, 1)], axis=0),
            lax.ppermute(slope, ("pipe", "dp", "tensor"), moves),
        )

    def second_half(arriving, back):
        d_up = (back * slope).astype(BF16)
        full_d_up = features_exchange(copies(d_up, parts))
        part = by_cols(full_d_up, up_w)
        mixed = add_blocks(chips_exchange(part))
        return (arriving.astype(F32) + mixed).astype(BF16), full_d_up, part

    def both_cores(x):
        return jnp.concatenate([x, swap_cores(x)], axis=0)

    def own_units(x):
        return jnp.concatenate([x[..., :units], swap_cores(x[..., units:])], axis=0)

    def own_hidden():
        return own_units(features_exchange(copies(hidden, parts)))

    def after(x, y):
        first = y[(0,) * y.ndim]
        return jnp.where(jnp.isnan(first), first, x)

    def weight_grads(all_in, all_hidden, full_back, full_d_up):
        grad_up = by_rows(all_in, own_units(full_d_up)).astype(BF16)
        grad_down = by_rows(all_hidden, both_cores(full_back)).astype(BF16)
        return grad_up, grad_down

    def tick(arriving):
        full_back = chips_exchange(copies(arriving, chips))
        back = add_blocks(features_exchange(by_cols(full_back, down_w)))
        out, full_d_up, part = second_half(arriving, back)
        return out, after(full_back, part), full_d_up

    def middle_tick(arriving):
        row_back = row_exchange(copies(arriving, few))
        part = jnp.concatenate([by_cols(row_back, down_w), by_cols(row_back, down_mate)], axis=0)
        back = add_blocks(features_exchange(part))
        d_up = (back * middle_slope).astype(BF16)
        row_d_up = features_exchange(copies(d_up, parts))
        part = cols_product(row_d_up[:few], up_w) + cols_product(row_d_up[few:], up_mate)
        mixed = add_blocks(row_exchange(part.astype(BF16)))
        return (arriving.astype(F32) + mixed).astype(BF16), row_back, row_d_up

    def own_row_first(x):
        x = x.reshape((few, 2) + x.shape[1:])
        first, second = x[:, 0], x[:, 1]
        return jnp.concatenate(
            [jnp.where(y_hi == 0, first, second), jnp.where(y_hi == 0, second, first)], axis=0
        )

    def middle_grads(row_back, row_d_up):
        all_back = jnp.concatenate([row_back, swap_mates(row_back, 2)], axis=0)
        all_d_up = jnp.concatenate([row_d_up[:few], swap_mates(row_d_up[few:], 2)], axis=0)
        all_hidden = own_units(own_row_first(features_exchange(copies(hidden, parts))))
        return weight_grads(both_cores(own_row_first(full_in)), all_hidden, all_back, all_d_up)

    def first_tick():
        return second_half(fresh, sums[block:])[:2]

    out, full_d_up = lax.cond(
        segment == last,
        first_tick,
        lambda: (jnp.zeros((block, width), BF16), jnp.zeros((parts, block, 2 * units), BF16)),
    )
    up_mate, down_mate, middle_slope = lax.cond(
        jnp.logical_and(segment > 0, segment < last),
        middle_weights,
        lambda: (jnp.zeros_like(up_w), jnp.zeros_like(down_w), jnp.zeros_like(slope)),
    )
    row_back = jnp.zeros((few, block, width), BF16)
    row_d_up = jnp.zeros((parts, block, 2 * units), BF16)
    for at in range(last - 1, 0, -1):
        received = lax.ppermute(out, "pipe", [(at + 1, at)])
        out, row_back, row_d_up = lax.cond(
            segment == at,
            lambda received, out, row_back, row_d_up: middle_tick(received),
            lambda received, out, row_back, row_d_up: (out, row_back, row_d_up),
            received,
            out,
            row_back,
            row_d_up,
        )
    all_in, all_hidden = lax.cond(
        segment == 0,
        lambda: (both_cores(full_in), own_hidden()),
        lambda: (
            jnp.zeros((2 * chips, block, width), BF16),
            jnp.zeros((2 * parts, block, units), BF16),
        ),
    )
    received = lax.ppermute(out, "pipe", [(1, 0)])

    def end_lowest():
        out, full_back, full_d_up = tick(received)
        return (out,) + weight_grads(all_in, all_hidden, full_back, full_d_up)

    def end_middle():
        return (out,) + middle_grads(row_back, row_d_up)

    def end_highest():
        return (out,) + weight_grads(both_cores(full_in), own_hidden(), full_back, full_d_up)

    which = jnp.where(segment == 0, 0, jnp.where(segment == last, 2, 1))
    out, grad_up, grad_down = lax.switch(which, (end_lowest, end_middle, end_highest))
    grads_in = jnp.swapaxes(out.reshape(rows, micro_count, width), 0, 1)
    return grads_in[None], grad_up[None], grad_down[None]


def solution(mesh):
    return jax.shard_map(
        body,
        mesh=mesh,
        in_specs=(
            P("pipe", None, "dp", "tensor"),
            P(None, "dp", "tensor"),
            P(),
            P("pipe", "tensor", "dp"),
            P("pipe", "dp", "tensor"),
        ),
        out_specs=(
            P("pipe", None, "dp", "tensor"),
            P("pipe", "tensor", "dp"),
            P("pipe", "dp", "tensor"),
        ),
        check_vma=False,
    )
```

```python
import functools

import jax
import jax.numpy as jnp
from jax import lax
from jax.sharding import PartitionSpec as P

BF16 = jnp.bfloat16
F32 = jnp.float32


def swap_cores(x):
    peers = lax.axis_size("dp")
    return lax.ppermute(x, "dp", [(i, i ^ 1) for i in range(peers)])


def chips_exchange(x):
    peers = lax.axis_size("dp")
    groups = [[i for i in range(peers) if i % 2 == core] for core in range(2)]
    return lax.all_to_all(x, "dp", 0, 0, axis_index_groups=groups, tiled=True)


def row_exchange(x):
    peers = lax.axis_size("dp")
    groups = [[4 * at + r for at in range(peers // 4)] for r in range(4)]
    return lax.all_to_all(x, "dp", 0, 0, axis_index_groups=groups, tiled=True)


def rows_from_above(x, at):
    segments, peers = lax.axis_size("pipe"), lax.axis_size("dp")
    few = peers // 4
    others = [p for p in range(segments) if p not in (at, at + 1)]
    groups = [
        [p * peers + 4 * k + r for p in two for k in range(few)]
        for two in ([at, at + 1], others)
        for r in range(4)
    ]
    x = lax.all_to_all(copies(x, 2 * few), ("pipe", "dp"), 0, 0, axis_index_groups=groups, tiled=True)
    return x[few:]


def swap_middle(x, mate):
    segments, peers = lax.axis_size("pipe"), lax.axis_size("dp")
    pairs = [(p * peers + i, p * peers + (i ^ mate)) for p in range(1, segments - 1) for i in range(peers)]
    return lax.ppermute(x, ("pipe", "dp"), pairs)


def swap_in_group(x, group, mate):
    peers = lax.axis_size("dp")
    pairs = [(group * peers + i, group * peers + (i ^ mate)) for i in range(peers)]
    return lax.ppermute(x, ("pipe", "dp"), pairs)


def swap_mates(x, mate):
    return lax.ppermute(x, "dp", [(i, i ^ mate) for i in range(lax.axis_size("dp"))])


def features_exchange(x):
    return lax.all_to_all(x, "tensor", 0, 0, tiled=True)


def copies(x, count):
    return jnp.broadcast_to(x[None], (count,) + x.shape)


def add_blocks(x):
    return jnp.sum(x.astype(F32), axis=0)


def cols_product(left, right):
    return lax.dot_general(
        left, right, (((left.ndim - 1,), (1,)), ((), ())), preferred_element_type=F32
    )


def by_cols(left, right):
    return cols_product(left, right).astype(BF16)


def by_rows(left, right):
    dims = tuple(range(left.ndim - 1))
    return lax.dot_general(left, right, ((dims, dims), ((), ())), preferred_element_type=F32)


def body(saved, pool, picked, w_up, w_down):
    segments = lax.axis_size("pipe")
    segment = lax.axis_index("pipe")
    chips = lax.axis_size("dp") // 2
    parts = lax.axis_size("tensor")
    micro_count, rows, width = saved.shape[1:]
    units = w_up.shape[2]
    block = micro_count * rows
    last = segments - 1
    peers = lax.axis_size("dp")
    few = chips // 2
    y_hi = (lax.axis_index("dp") // 2) % 2

    up_w = jnp.concatenate([w_up[0], swap_cores(w_up[0])], axis=1)
    down_w = jnp.concatenate([w_down[0], swap_cores(w_down[0])], axis=0)

    up_other = swap_middle(w_up[0], 2)
    down_other = swap_middle(w_down[0], 2)

    samples = jnp.swapaxes(pool, 0, 1)
    fresh = jnp.zeros((rows, micro_count, width), BF16)
    for sample in range(pool.shape[0]):
        fresh = jnp.where((picked == sample)[None, :, None], samples[:, sample][:, None], fresh)
    fresh = fresh.reshape(block, width)
    inputs = jnp.swapaxes(saved[0], 0, 1).reshape(block, width)

    gathered = chips_exchange(copies(jnp.concatenate([inputs, fresh], axis=0), chips))
    full_in = gathered[:, :block]
    full_back = gathered[:, block:]
    up_part = lax.dot_general(
        full_in, up_w, (((2,), (0,)), ((), ())), preferred_element_type=F32
    ).astype(BF16)
    back_part = by_cols(full_back, down_w)
    sums = add_blocks(features_exchange(jnp.concatenate([up_part, back_part], axis=1)))
    up = sums[:block]
    sig = jax.nn.sigmoid(up)
    hidden = (up * sig).astype(BF16)
    slope = sig * (1.0 + up * (1.0 - sig))

    moves = []
    for group in range(1, last):
        for i in range(peers):
            for z in range(parts):
                units_y, tokens_y = (i // 2) % 2, z % 2
                to = i - 2 * units_y + 2 * tokens_y
                place = (units_y ^ tokens_y) * few + z // 2
                moves.append(((group * peers + i) * parts + z, (group * peers + to) * parts + place))


    def second_half(arriving, back):
        d_up = (back * slope).astype(BF16)
        full_d_up = features_exchange(copies(d_up, parts))
        part = by_cols(full_d_up, up_w)
        mixed = add_blocks(chips_exchange(part))
        return (arriving.astype(F32) + mixed).astype(BF16), full_d_up, part

    def both_cores(x):
        return jnp.concatenate([x, swap_cores(x)], axis=0)

    def own_units(x):
        return jnp.concatenate([x[..., :units], swap_cores(x[..., units:])], axis=0)

    def own_hidden():
        return own_units(features_exchange(copies(hidden, parts)))

    def after(x, y):
        return jnp.where(jnp.isnan(y), y, x)

    def weight_grads(all_in, all_hidden, full_back, full_d_up):
        grad_up = by_rows(all_in, own_units(full_d_up)).astype(BF16)
        grad_down = by_rows(all_hidden, both_cores(full_back)).astype(BF16)
        return grad_up, grad_down

    def tick(arriving):
        full_back = chips_exchange(copies(arriving, chips))
        back = add_blocks(features_exchange(by_cols(full_back, down_w)))
        out, full_d_up, part = second_half(arriving, back)
        return out, after(full_back, part), full_d_up

    def middle_tick(at, row_back):
        up_mate = jnp.concatenate([up_other, swap_in_group(up_other, at, 1)], axis=1)
        arriving = lax.dynamic_index_in_dim(row_back, lax.axis_index("dp") // 4, 0, keepdims=False)
        part = jnp.concatenate([by_cols(row_back, down_w), by_cols(row_back, down_mate)], axis=0)
        back = add_blocks(features_exchange(part))
        d_up = (back * middle_slope).astype(BF16)
        row_d_up = features_exchange(copies(d_up, parts))
        part = cols_product(row_d_up[:few], up_w) + cols_product(row_d_up[few:], up_mate)
        mixed = add_blocks(row_exchange(part.astype(BF16)))
        return (arriving.astype(F32) + mixed).astype(BF16), row_d_up

    def own_row_first(x):
        x = x.reshape((few, 2) + x.shape[1:])
        first, second = x[:, 0], x[:, 1]
        return jnp.concatenate(
            [jnp.where(y_hi == 0, first, second), jnp.where(y_hi == 0, second, first)], axis=0
        )

    def middle_grads(row_back, row_d_up):
        full_hidden = features_exchange(copies(hidden, parts))
        row_d_up = after(row_d_up, full_hidden)
        row_back = after(row_back, full_hidden[:few, :, :width])
        all_back = jnp.concatenate([row_back, swap_mates(row_back, 2)], axis=0)
        all_d_up = jnp.concatenate([row_d_up[:few], swap_mates(row_d_up[few:], 2)], axis=0)
        all_hidden = own_units(own_row_first(full_hidden))
        return weight_grads(both_cores(own_row_first(full_in)), all_hidden, all_back, all_d_up)

    def first_tick():
        return second_half(fresh, sums[block:])[:2] + (jnp.zeros(slope.shape, BF16),)

    down_mate = lax.cond(
        jnp.logical_and(segment > 0, segment < last),
        lambda: jnp.concatenate([down_other, swap_middle(down_other, 1)], axis=0),
        lambda: jnp.zeros_like(down_w),
    )

    def skip_first():
        moved = lax.ppermute(slope.astype(BF16), ("pipe", "dp", "tensor"), moves)
        return down_mate[:block], jnp.zeros((parts, block, 2 * units), BF16), moved

    out, full_d_up, middle_slope = lax.cond(segment == last, first_tick, skip_first)
    outs, kept_back, kept_d_up = [out], [], []
    for at in range(last - 1, 0, -1):
        row_back = rows_from_above(out, at)
        out, row_d_up = lax.cond(
            segment == at,
            functools.partial(middle_tick, at),
            lambda row_back: (
                jnp.zeros((block, width), BF16),
                jnp.zeros((parts, block, 2 * units), BF16),
            ),
            row_back,
        )
        outs.append(out)
        kept_back.append(row_back)
        kept_d_up.append(row_d_up)
    all_in, all_hidden = lax.cond(
        segment == 0,
        lambda: (both_cores(full_in), own_hidden()),
        lambda: (
            jnp.zeros((2 * chips, block, width), BF16),
            jnp.zeros((2 * parts, block, units), BF16),
        ),
    )
    received = lax.ppermute(out, "pipe", [(1, 0)])

    def end_lowest():
        out, full_back, full_d_up = tick(received)
        return (out,) + weight_grads(all_in, all_hidden, full_back, full_d_up)

    def end_middle(k):
        return lambda: (outs[k + 1],) + middle_grads(kept_back[k], kept_d_up[k])

    def end_highest():
        return (outs[0],) + weight_grads(both_cores(full_in), own_hidden(), full_back, full_d_up)

    ends = [end_lowest] + [end_middle(last - 1 - at) for at in range(1, last)] + [end_highest]
    out, grad_up, grad_down = lax.switch(segment, ends)
    grads_in = jnp.swapaxes(out.reshape(rows, micro_count, width), 0, 1)
    return grads_in[None], grad_up[None], grad_down[None]


def solution(mesh):
    return jax.shard_map(
        body,
        mesh=mesh,
        in_specs=(
            P("pipe", None, "dp", "tensor"),
            P(None, "dp", "tensor"),
            P(),
            P("pipe", "tensor", "dp"),
            P("pipe", "dp", "tensor"),
        ),
        out_specs=(
            P("pipe", None, "dp", "tensor"),
            P("pipe", "tensor", "dp"),
            P("pipe", "dp", "tensor"),
        ),
        check_vma=False,
    )
```

```python
import functools

import jax
import jax.numpy as jnp
from jax import lax
from jax.sharding import PartitionSpec as P

BF16 = jnp.bfloat16
F32 = jnp.float32


def swap_cores(x):
    peers = lax.axis_size("dp")
    return lax.ppermute(x, "dp", [(i, i ^ 1) for i in range(peers)])


def chips_exchange(x):
    peers = lax.axis_size("dp")
    groups = [[i for i in range(peers) if i % 2 == core] for core in range(2)]
    return lax.all_to_all(x, "dp", 0, 0, axis_index_groups=groups, tiled=True)


def row_exchange(x):
    peers = lax.axis_size("dp")
    groups = [[4 * at + r for at in range(peers // 4)] for r in range(4)]
    return lax.all_to_all(x, "dp", 0, 0, axis_index_groups=groups, tiled=True)


def rows_from_above(x, at):
    segments, peers = lax.axis_size("pipe"), lax.axis_size("dp")
    few = peers // 4
    others = [p for p in range(segments) if p not in (at, at + 1)]
    groups = [
        [p * peers + 4 * k + r for p in two for k in range(few)]
        for two in ([at, at + 1], others)
        for r in range(4)
    ]
    x = lax.all_to_all(copies(x, 2 * few), ("pipe", "dp"), 0, 0, axis_index_groups=groups, tiled=True)
    return x[few:]


def swap_middle(x, mate):
    segments, peers = lax.axis_size("pipe"), lax.axis_size("dp")
    pairs = [(p * peers + i, p * peers + (i ^ mate)) for p in range(1, segments - 1) for i in range(peers)]
    return lax.ppermute(x, ("pipe", "dp"), pairs)


def swap_in_group(x, group, mate):
    peers = lax.axis_size("dp")
    pairs = [(group * peers + i, group * peers + (i ^ mate)) for i in range(peers)]
    return lax.ppermute(x, ("pipe", "dp"), pairs)


def swap_mates(x, mate):
    return lax.ppermute(x, "dp", [(i, i ^ mate) for i in range(lax.axis_size("dp"))])


def features_exchange(x):
    return lax.all_to_all(x, "tensor", 0, 0, tiled=True)


def copies(x, count):
    return jnp.broadcast_to(x[None], (count,) + x.shape)


def add_blocks(x):
    return jnp.sum(x.astype(F32), axis=0)


def cols_product(left, right):
    return lax.dot_general(
        left, right, (((left.ndim - 1,), (1,)), ((), ())), preferred_element_type=F32
    )


def by_cols(left, right):
    return cols_product(left, right).astype(BF16)


def by_rows(left, right):
    dims = tuple(range(left.ndim - 1))
    return lax.dot_general(left, right, ((dims, dims), ((), ())), preferred_element_type=F32)


def body(saved, pool, picked, w_up, w_down):
    segments = lax.axis_size("pipe")
    segment = lax.axis_index("pipe")
    chips = lax.axis_size("dp") // 2
    parts = lax.axis_size("tensor")
    micro_count, rows, width = saved.shape[1:]
    units = w_up.shape[2]
    block = micro_count * rows
    last = segments - 1
    peers = lax.axis_size("dp")
    few = chips // 2
    y_hi = (lax.axis_index("dp") // 2) % 2

    up_w = jnp.concatenate([w_up[0], swap_cores(w_up[0])], axis=1)
    down_w = jnp.concatenate([w_down[0], swap_cores(w_down[0])], axis=0)

    up_other = swap_middle(w_up[0], 2)
    down_other = swap_middle(w_down[0], 2)

    samples = jnp.swapaxes(pool, 0, 1)
    fresh = jnp.zeros((rows, micro_count, width), BF16)
    for sample in range(pool.shape[0]):
        fresh = jnp.where((picked == sample)[None, :, None], samples[:, sample][:, None], fresh)
    fresh = fresh.reshape(block, width)
    inputs = jnp.swapaxes(saved[0], 0, 1).reshape(block, width)

    gathered = chips_exchange(copies(jnp.concatenate([inputs, fresh], axis=0), chips))
    full_in = gathered[:, :block]
    full_back = gathered[:, block:]
    up_part = lax.dot_general(
        full_in, up_w, (((2,), (0,)), ((), ())), preferred_element_type=F32
    ).astype(BF16)
    back_part = by_cols(full_back, down_w)
    sums = add_blocks(features_exchange(jnp.concatenate([up_part, back_part], axis=1)))
    up = sums[:block]
    sig = jax.nn.sigmoid(up)
    hidden = (up * sig).astype(BF16)
    slope = sig * (1.0 + up * (1.0 - sig))

    moves = []
    for group in range(1, last):
        for i in range(peers):
            for z in range(parts):
                units_y, tokens_y = (i // 2) % 2, z % 2
                to = i - 2 * units_y + 2 * tokens_y
                place = (units_y ^ tokens_y) * few + z // 2
                moves.append(((group * peers + i) * parts + z, (group * peers + to) * parts + place))


    def second_half(arriving, back, stagger=False):
        d_up = (back * slope).astype(BF16)
        if stagger:
            pairs = [(last * peers + i, last * peers + (i ^ 4)) for i in range(0, peers, 2)]
            step = lax.ppermute(d_up, ("pipe", "dp"), pairs)
            d_up = after(d_up, step)
        full_d_up = features_exchange(copies(d_up, parts))
        part = by_cols(full_d_up, up_w)
        mixed = add_blocks(chips_exchange(part))
        return (arriving.astype(F32) + mixed).astype(BF16), full_d_up, part

    def both_cores(x):
        return jnp.concatenate([x, swap_cores(x)], axis=0)

    def own_units(x):
        return jnp.concatenate([x[..., :units], swap_cores(x[..., units:])], axis=0)

    def own_hidden():
        return own_units(features_exchange(copies(hidden, parts)))

    def after(x, y):
        return jnp.where(jnp.isnan(y), y, x)

    def weight_products(all_in, all_hidden, all_back, full_d_up):
        grad_up = by_rows(all_in, own_units(full_d_up)).astype(BF16)
        grad_down = by_rows(all_hidden, all_back).astype(BF16)
        return grad_up, grad_down

    def weight_grads(all_in, all_hidden, full_back, full_d_up):
        return weight_products(all_in, all_hidden, both_cores(full_back), full_d_up)

    def tick(arriving):
        full_back = chips_exchange(copies(arriving, chips))
        back = add_blocks(features_exchange(by_cols(full_back, down_w)))
        out, full_d_up, part = second_half(arriving, back)
        return out, full_back, full_d_up, part

    def middle_tick(at, row_back):
        up_mate = jnp.concatenate([up_other, swap_in_group(up_other, at, 1)], axis=1)
        arriving = lax.dynamic_index_in_dim(row_back, lax.axis_index("dp") // 4, 0, keepdims=False)
        part = jnp.concatenate([by_cols(row_back, down_w), by_cols(row_back, down_mate)], axis=0)
        back = add_blocks(features_exchange(part))
        d_up = (back * middle_slope).astype(BF16)
        row_d_up = features_exchange(copies(d_up, parts))
        part = cols_product(row_d_up[:few], up_w) + cols_product(row_d_up[few:], up_mate)
        mixed = add_blocks(row_exchange(part.astype(BF16)))
        return (arriving.astype(F32) + mixed).astype(BF16), row_d_up

    def own_row_first(x):
        x = x.reshape((few, 2) + x.shape[1:])
        first, second = x[:, 0], x[:, 1]
        return jnp.concatenate(
            [jnp.where(y_hi == 0, first, second), jnp.where(y_hi == 0, second, first)], axis=0
        )

    def middle_grads(row_back, row_d_up):
        full_hidden = features_exchange(copies(hidden, parts))
        row_d_up = after(row_d_up, full_hidden)
        row_back = after(row_back, full_hidden[:few, :, :width])
        all_back = jnp.concatenate([row_back, swap_mates(row_back, 2)], axis=0)
        all_d_up = jnp.concatenate([row_d_up[:few], swap_mates(row_d_up[few:], 2)], axis=0)
        all_hidden = own_units(own_row_first(full_hidden))
        return weight_grads(both_cores(own_row_first(full_in)), all_hidden, all_back, all_d_up)

    def first_tick():
        return second_half(fresh, sums[block:], True)[:2] + (jnp.zeros(slope.shape, BF16),)

    down_mate = lax.cond(
        jnp.logical_and(segment > 0, segment < last),
        lambda: jnp.concatenate([down_other, swap_middle(down_other, 1)], axis=0),
        lambda: jnp.zeros_like(down_w),
    )

    def skip_first():
        moved = lax.ppermute(slope.astype(BF16), ("pipe", "dp", "tensor"), moves)
        return down_mate[:block], jnp.zeros((parts, block, 2 * units), BF16), moved

    out, full_d_up, middle_slope = lax.cond(segment == last, first_tick, skip_first)
    outs, kept_back, kept_d_up = [out], [], []
    for at in range(last - 1, 0, -1):
        row_back = rows_from_above(out, at)
        out, row_d_up = lax.cond(
            segment == at,
            functools.partial(middle_tick, at),
            lambda row_back: (
                jnp.zeros((block, width), BF16),
                jnp.zeros((parts, block, 2 * units), BF16),
            ),
            row_back,
        )
        outs.append(out)
        kept_back.append(row_back)
        kept_d_up.append(row_d_up)
    all_in, all_hidden = lax.cond(
        segment == 0,
        lambda: (both_cores(full_in), own_hidden()),
        lambda: (
            jnp.zeros((2 * chips, block, width), BF16),
            jnp.zeros((2 * parts, block, units), BF16),
        ),
    )
    received = lax.ppermute(out, "pipe", [(1, 0)])

    def end_lowest():
        out, full_back, full_d_up, part = tick(received)
        held = after(full_back[:1], part[:1])
        all_back = jnp.concatenate([held, full_back[1:], swap_cores(full_back)], axis=0)
        return (out,) + weight_products(all_in, all_hidden, all_back, full_d_up)

    def end_middle(k):
        return lambda: (outs[k + 1],) + middle_grads(kept_back[k], kept_d_up[k])

    def end_highest():
        return (outs[0],) + weight_grads(both_cores(full_in), own_hidden(), full_back, full_d_up)

    ends = [end_lowest] + [end_middle(last - 1 - at) for at in range(1, last)] + [end_highest]
    out, grad_up, grad_down = lax.switch(segment, ends)
    grads_in = jnp.swapaxes(out.reshape(rows, micro_count, width), 0, 1)
    return grads_in[None], grad_up[None], grad_down[None]


def solution(mesh):
    return jax.shard_map(
        body,
        mesh=mesh,
        in_specs=(
            P("pipe", None, "dp", "tensor"),
            P(None, "dp", "tensor"),
            P(),
            P("pipe", "tensor", "dp"),
            P("pipe", "dp", "tensor"),
        ),
        out_specs=(
            P("pipe", None, "dp", "tensor"),
            P("pipe", "tensor", "dp"),
            P("pipe", "dp", "tensor"),
        ),
        check_vma=False,
    )
```

```python
import functools

import jax
import jax.numpy as jnp
from jax import lax
from jax.sharding import PartitionSpec as P

BF16 = jnp.bfloat16
F32 = jnp.float32


def swap_cores(x):
    peers = lax.axis_size("dp")
    return lax.ppermute(x, "dp", [(i, i ^ 1) for i in range(peers)])


def chips_exchange(x):
    peers = lax.axis_size("dp")
    groups = [[i for i in range(peers) if i % 2 == core] for core in range(2)]
    return lax.all_to_all(x, "dp", 0, 0, axis_index_groups=groups, tiled=True)


def row_exchange(x):
    peers = lax.axis_size("dp")
    groups = [[4 * at + r for at in range(peers // 4)] for r in range(4)]
    return lax.all_to_all(x, "dp", 0, 0, axis_index_groups=groups, tiled=True)


def rows_from_above(x, at):
    segments, peers = lax.axis_size("pipe"), lax.axis_size("dp")
    few = peers // 4
    others = [p for p in range(segments) if p not in (at, at + 1)]
    groups = [
        [p * peers + 4 * k + r for p in two for k in range(few)]
        for two in ([at, at + 1], others)
        for r in range(4)
    ]
    x = lax.all_to_all(copies(x, 2 * few), ("pipe", "dp"), 0, 0, axis_index_groups=groups, tiled=True)
    return x[few:]


def row_sums_from_above(x, at):
    got = rows_from_above(x.reshape((-1,) + x.shape[2:]), at)
    return add_blocks(got).astype(BF16).reshape(x.shape)


def swap_middle(x, mate):
    segments, peers = lax.axis_size("pipe"), lax.axis_size("dp")
    pairs = [(p * peers + i, p * peers + (i ^ mate)) for p in range(1, segments - 1) for i in range(peers)]
    return lax.ppermute(x, ("pipe", "dp"), pairs)


def swap_in_group(x, group, mate):
    peers = lax.axis_size("dp")
    pairs = [(group * peers + i, group * peers + (i ^ mate)) for i in range(peers)]
    return lax.ppermute(x, ("pipe", "dp"), pairs)


def swap_mates(x, mate):
    return lax.ppermute(x, "dp", [(i, i ^ mate) for i in range(lax.axis_size("dp"))])


def features_exchange(x):
    return lax.all_to_all(x, "tensor", 0, 0, tiled=True)


def copies(x, count):
    return jnp.broadcast_to(x[None], (count,) + x.shape)


def add_blocks(x):
    return jnp.sum(x.astype(F32), axis=0)


def cols_product(left, right):
    return lax.dot_general(
        left, right, (((left.ndim - 1,), (1,)), ((), ())), preferred_element_type=F32
    )


def by_cols(left, right):
    return cols_product(left, right).astype(BF16)


def by_rows(left, right):
    dims = tuple(range(left.ndim - 1))
    return lax.dot_general(left, right, ((dims, dims), ((), ())), preferred_element_type=F32)


def body(saved, pool, picked, w_up, w_down):
    segments = lax.axis_size("pipe")
    segment = lax.axis_index("pipe")
    chips = lax.axis_size("dp") // 2
    parts = lax.axis_size("tensor")
    micro_count, rows, width = saved.shape[1:]
    units = w_up.shape[2]
    block = micro_count * rows
    last = segments - 1
    peers = lax.axis_size("dp")
    few = chips // 2
    y_hi = (lax.axis_index("dp") // 2) % 2

    up_w = jnp.concatenate([w_up[0], swap_cores(w_up[0])], axis=1)
    down_w = jnp.concatenate([w_down[0], swap_cores(w_down[0])], axis=0)

    up_other = swap_middle(w_up[0], 2)
    down_other = swap_middle(w_down[0], 2)

    samples = jnp.swapaxes(pool, 0, 1)
    fresh = jnp.zeros((rows, micro_count, width), BF16)
    for sample in range(pool.shape[0]):
        fresh = jnp.where((picked == sample)[None, :, None], samples[:, sample][:, None], fresh)
    fresh = fresh.reshape(block, width)
    inputs = jnp.swapaxes(saved[0], 0, 1).reshape(block, width)

    gathered = chips_exchange(copies(jnp.concatenate([inputs, fresh], axis=0), chips))
    full_in = gathered[:, :block]
    full_back = gathered[:, block:]
    up_part = lax.dot_general(
        full_in, up_w, (((2,), (0,)), ((), ())), preferred_element_type=F32
    ).astype(BF16)
    back_part = by_cols(full_back, down_w)
    sums = add_blocks(features_exchange(jnp.concatenate([up_part, back_part], axis=1)))
    up = sums[:block]
    sig = jax.nn.sigmoid(up)
    hidden = (up * sig).astype(BF16)
    slope = sig * (1.0 + up * (1.0 - sig))

    moves = []
    for group in range(1, last):
        for i in range(peers):
            for z in range(parts):
                units_y, tokens_y = (i // 2) % 2, z % 2
                to = i - 2 * units_y + 2 * tokens_y
                place = (units_y ^ tokens_y) * few + z // 2
                moves.append(((group * peers + i) * parts + z, (group * peers + to) * parts + place))


    def second_half(arriving, back, stagger=False):
        d_up = (back * slope).astype(BF16)
        if stagger:
            pairs = [(last * peers + i, last * peers + (i ^ 4)) for i in range(0, peers, 2)]
            step = lax.ppermute(d_up, ("pipe", "dp"), pairs)
            d_up = after(d_up, step)
        full_d_up = features_exchange(copies(d_up, parts))
        part = by_cols(full_d_up, up_w)
        mixed = add_blocks(chips_exchange(part))
        return (arriving.astype(F32) + mixed).astype(BF16), full_d_up, part

    def both_cores(x):
        return jnp.concatenate([x, swap_cores(x)], axis=0)

    def own_units(x):
        return jnp.concatenate([x[..., :units], swap_cores(x[..., units:])], axis=0)

    def own_hidden():
        return own_units(features_exchange(copies(hidden, parts)))

    def after(x, y):
        return jnp.where(jnp.isnan(y), y, x)

    def weight_products(all_in, all_hidden, all_back, full_d_up):
        grad_up = by_rows(all_in, own_units(full_d_up)).astype(BF16)
        grad_down = by_rows(all_hidden, all_back).astype(BF16)
        return grad_up, grad_down

    def weight_grads(all_in, all_hidden, full_back, full_d_up):
        return weight_products(all_in, all_hidden, both_cores(full_back), full_d_up)

    def tick(arriving):
        full_back = chips_exchange(copies(arriving, chips))
        back = add_blocks(features_exchange(by_cols(full_back, down_w)))
        out, full_d_up, part = second_half(arriving, back)
        return out, full_back, full_d_up, part

    def middle_tick(at, row_back):
        row = lax.axis_index("dp") // 4
        up_mate = jnp.concatenate([up_other, swap_in_group(up_other, at, 1)], axis=1)
        arriving = lax.dynamic_index_in_dim(row_back, row, 0, keepdims=False)
        part = jnp.concatenate([by_cols(row_back, down_w), by_cols(row_back, down_mate)], axis=0)
        back = add_blocks(features_exchange(part))
        d_up = (back * middle_slope).astype(BF16)
        row_d_up = features_exchange(copies(d_up, parts))
        part = cols_product(row_d_up[:few], up_w) + cols_product(row_d_up[few:], up_mate)
        if at == last - 1:
            mine = jnp.arange(few)[:, None, None] == row
            return (part + jnp.where(mine, row_back.astype(F32), 0.0)).astype(BF16), row_d_up
        mixed = add_blocks(row_exchange(part.astype(BF16)))
        return (arriving.astype(F32) + mixed).astype(BF16), row_d_up

    def own_row_first(x):
        x = x.reshape((few, 2) + x.shape[1:])
        first, second = x[:, 0], x[:, 1]
        return jnp.concatenate(
            [jnp.where(y_hi == 0, first, second), jnp.where(y_hi == 0, second, first)], axis=0
        )

    def middle_grads(row_back, row_d_up):
        full_hidden = features_exchange(copies(hidden, parts))
        row_d_up = after(row_d_up, full_hidden)
        row_back = after(row_back, full_hidden[:few, :, :width])
        all_back = jnp.concatenate([row_back, swap_mates(row_back, 2)], axis=0)
        all_d_up = jnp.concatenate([row_d_up[:few], swap_mates(row_d_up[few:], 2)], axis=0)
        all_hidden = own_units(own_row_first(full_hidden))
        return weight_grads(both_cores(own_row_first(full_in)), all_hidden, all_back, all_d_up)

    def first_tick():
        return second_half(fresh, sums[block:], True)[:2] + (jnp.zeros(slope.shape, BF16),)

    down_mate = lax.cond(
        jnp.logical_and(segment > 0, segment < last),
        lambda: jnp.concatenate([down_other, swap_middle(down_other, 1)], axis=0),
        lambda: jnp.zeros_like(down_w),
    )

    def skip_first():
        moved = lax.ppermute(slope.astype(BF16), ("pipe", "dp", "tensor"), moves)
        return down_mate[:block], jnp.zeros((parts, block, 2 * units), BF16), moved

    out, full_d_up, middle_slope = lax.cond(segment == last, first_tick, skip_first)
    outs, kept_back, kept_d_up = [out], [], []
    for at in range(last - 1, 0, -1):
        if at == last - 1:
            row_back = rows_from_above(out, at)
            shape = row_back.shape
        else:
            row_back = row_sums_from_above(out, at)
            outs.append(lax.dynamic_index_in_dim(row_back, lax.axis_index("dp") // 4, 0, keepdims=False))
            shape = (block, width)
        out, row_d_up = lax.cond(
            segment == at,
            functools.partial(middle_tick, at),
            lambda row_back, shape=shape: (
                jnp.zeros(shape, BF16),
                jnp.zeros((parts, block, 2 * units), BF16),
            ),
            row_back,
        )
        kept_back.append(row_back)
        kept_d_up.append(row_d_up)
    outs.append(out)
    all_in, all_hidden = lax.cond(
        segment == 0,
        lambda: (both_cores(full_in), own_hidden()),
        lambda: (
            jnp.zeros((2 * chips, block, width), BF16),
            jnp.zeros((2 * parts, block, units), BF16),
        ),
    )
    received = lax.ppermute(out, "pipe", [(1, 0)])

    def end_lowest():
        out, full_back, full_d_up, part = tick(received)
        held = after(full_back[:1], part[:1])
        all_back = jnp.concatenate([held, full_back[1:], swap_cores(full_back)], axis=0)
        return (out,) + weight_products(all_in, all_hidden, all_back, full_d_up)

    def end_middle(k):
        return lambda: (outs[k + 1],) + middle_grads(kept_back[k], kept_d_up[k])

    def end_highest():
        return (outs[0],) + weight_grads(both_cores(full_in), own_hidden(), full_back, full_d_up)

    ends = [end_lowest] + [end_middle(last - 1 - at) for at in range(1, last)] + [end_highest]
    out, grad_up, grad_down = lax.switch(segment, ends)
    grads_in = jnp.swapaxes(out.reshape(rows, micro_count, width), 0, 1)
    return grads_in[None], grad_up[None], grad_down[None]


def solution(mesh):
    return jax.shard_map(
        body,
        mesh=mesh,
        in_specs=(
            P("pipe", None, "dp", "tensor"),
            P(None, "dp", "tensor"),
            P(),
            P("pipe", "tensor", "dp"),
            P("pipe", "dp", "tensor"),
        ),
        out_specs=(
            P("pipe", None, "dp", "tensor"),
            P("pipe", "tensor", "dp"),
            P("pipe", "dp", "tensor"),
        ),
        check_vma=False,
    )
```

```python
import functools

import jax
import jax.numpy as jnp
from jax import lax
from jax.sharding import PartitionSpec as P

BF16 = jnp.bfloat16
F32 = jnp.float32


def swap_cores(x):
    peers = lax.axis_size("dp")
    return lax.ppermute(x, "dp", [(i, i ^ 1) for i in range(peers)])


def chips_exchange(x):
    peers = lax.axis_size("dp")
    groups = [[i for i in range(peers) if i % 2 == core] for core in range(2)]
    return lax.all_to_all(x, "dp", 0, 0, axis_index_groups=groups, tiled=True)


def row_exchange(x):
    peers = lax.axis_size("dp")
    groups = [[4 * at + r for at in range(peers // 4)] for r in range(4)]
    return lax.all_to_all(x, "dp", 0, 0, axis_index_groups=groups, tiled=True)


def rows_from_above(x, at):
    segments, peers = lax.axis_size("pipe"), lax.axis_size("dp")
    few = peers // 4
    others = [p for p in range(segments) if p not in (at, at + 1)]
    groups = [
        [p * peers + 4 * k + r for p in two for k in range(few)]
        for two in ([at, at + 1], others)
        for r in range(4)
    ]
    x = lax.all_to_all(copies(x, 2 * few), ("pipe", "dp"), 0, 0, axis_index_groups=groups, tiled=True)
    return x[few:]


def row_sums_from_above(x, at):
    got = rows_from_above(x.reshape((-1,) + x.shape[2:]), at)
    return add_blocks(got).astype(BF16).reshape(x.shape)


def swap_middle(x, mate):
    segments, peers = lax.axis_size("pipe"), lax.axis_size("dp")
    pairs = [(p * peers + i, p * peers + (i ^ mate)) for p in range(1, segments - 1) for i in range(peers)]
    return lax.ppermute(x, ("pipe", "dp"), pairs)


def swap_in_group(x, group, mate):
    peers = lax.axis_size("dp")
    pairs = [(group * peers + i, group * peers + (i ^ mate)) for i in range(peers)]
    return lax.ppermute(x, ("pipe", "dp"), pairs)


def swap_mates(x, mate):
    return lax.ppermute(x, "dp", [(i, i ^ mate) for i in range(lax.axis_size("dp"))])


def features_exchange(x):
    return lax.all_to_all(x, "tensor", 0, 0, tiled=True)


def copies(x, count):
    return jnp.broadcast_to(x[None], (count,) + x.shape)


def add_blocks(x):
    return jnp.sum(x.astype(F32), axis=0)


def cols_product(left, right):
    return lax.dot_general(
        left, right, (((left.ndim - 1,), (1,)), ((), ())), preferred_element_type=F32
    )


def by_cols(left, right):
    return cols_product(left, right).astype(BF16)


def by_rows(left, right):
    dims = tuple(range(left.ndim - 1))
    return lax.dot_general(left, right, ((dims, dims), ((), ())), preferred_element_type=F32)


def body(saved, pool, picked, w_up, w_down):
    segments = lax.axis_size("pipe")
    segment = lax.axis_index("pipe")
    chips = lax.axis_size("dp") // 2
    parts = lax.axis_size("tensor")
    micro_count, rows, width = saved.shape[1:]
    units = w_up.shape[2]
    block = micro_count * rows
    last = segments - 1
    peers = lax.axis_size("dp")
    few = chips // 2
    y_hi = (lax.axis_index("dp") // 2) % 2

    up_w = jnp.concatenate([w_up[0], swap_cores(w_up[0])], axis=1)
    down_w = jnp.concatenate([w_down[0], swap_cores(w_down[0])], axis=0)

    up_other = swap_in_group(w_up[0], last - 1, 2)
    up_other_low = swap_in_group(w_up[0], last - 2, 2)
    down_other = swap_middle(w_down[0], 2)

    samples = jnp.swapaxes(pool, 0, 1)
    fresh = jnp.zeros((rows, micro_count, width), BF16)
    for sample in range(pool.shape[0]):
        fresh = jnp.where((picked == sample)[None, :, None], samples[:, sample][:, None], fresh)
    fresh = fresh.reshape(block, width)
    inputs = jnp.swapaxes(saved[0], 0, 1).reshape(block, width)

    gathered = chips_exchange(copies(jnp.concatenate([inputs, fresh], axis=0), chips))
    full_in = gathered[:, :block]
    full_back = gathered[:, block:]
    up_part = lax.dot_general(
        full_in, up_w, (((2,), (0,)), ((), ())), preferred_element_type=F32
    ).astype(BF16)
    back_part = by_cols(full_back, down_w)
    sums = add_blocks(features_exchange(jnp.concatenate([up_part, back_part], axis=1)))
    up = sums[:block]
    sig = jax.nn.sigmoid(up)
    hidden = (up * sig).astype(BF16)
    slope = sig * (1.0 + up * (1.0 - sig))

    moves = []
    for group in range(1, last):
        for i in range(peers):
            for z in range(parts):
                units_y, tokens_y = (i // 2) % 2, z % 2
                to = i - 2 * units_y + 2 * tokens_y
                place = (units_y ^ tokens_y) * few + z // 2
                moves.append(((group * peers + i) * parts + z, (group * peers + to) * parts + place))


    def after(x, y):
        return jnp.where(jnp.isnan(y), y, x)

    def second_half(arriving, back, stagger=False):
        d_up = (back * slope).astype(BF16)
        if stagger:
            pairs = [(last * peers + i, last * peers + (i ^ 4)) for i in range(0, peers, 2)]
            step = lax.ppermute(d_up, ("pipe", "dp"), pairs)
            d_up = after(d_up, step)
        full_d_up = features_exchange(copies(d_up, parts))
        part = by_cols(full_d_up, up_w)
        mixed = add_blocks(chips_exchange(part))
        return (arriving.astype(F32) + mixed).astype(BF16), full_d_up, part

    def both_cores(x):
        return jnp.concatenate([x, swap_cores(x)], axis=0)

    def own_units(x):
        return jnp.concatenate([x[..., :units], swap_cores(x[..., units:])], axis=0)

    def own_hidden():
        return own_units(features_exchange(copies(hidden, parts)))

    def weight_products(all_in, all_hidden, all_back, all_d_up):
        grad_up = by_rows(all_in, all_d_up).astype(BF16)
        grad_down = by_rows(all_hidden, all_back).astype(BF16)
        return grad_up, grad_down

    def weight_grads(all_in, all_hidden, full_back, full_d_up):
        return weight_products(all_in, all_hidden, both_cores(full_back), own_units(full_d_up))

    def one_step_later(x):
        return after(x, lax.ppermute(x, ("pipe", "dp"), [(i, i ^ 4) for i in range(1, peers, 2)]))

    def tick(arriving):
        sent = lax.cond(lax.axis_index("dp") % 2 == 1, one_step_later, lambda x: x, arriving)
        full_back = chips_exchange(copies(sent, chips))
        back = add_blocks(features_exchange(by_cols(full_back, down_w)))
        out, full_d_up, part = second_half(arriving, back)
        return out, full_back, full_d_up, part

    def middle_tick(at, row_back):
        row = lax.axis_index("dp") // 4
        if at == last - 1:
            up_mate = jnp.concatenate([up_other, swap_in_group(up_other, at, 1)], axis=1)
        else:
            up_mate = up_mate_low
        arriving = lax.dynamic_index_in_dim(row_back, row, 0, keepdims=False)
        part = jnp.concatenate([by_cols(row_back, down_w), by_cols(row_back, down_mate)], axis=0)
        back = add_blocks(features_exchange(part))
        d_up = (back * middle_slope).astype(BF16)
        row_d_up = features_exchange(copies(d_up, parts))
        part = cols_product(row_d_up[:few], up_w) + cols_product(row_d_up[few:], up_mate)
        if at == last - 1:
            mine = jnp.arange(few)[:, None, None] == row
            return (part + jnp.where(mine, row_back.astype(F32), 0.0)).astype(BF16), row_d_up
        mixed = add_blocks(row_exchange(part.astype(BF16)))
        return (arriving.astype(F32) + mixed).astype(BF16), row_d_up

    def own_row_first(x):
        x = x.reshape((few, 2) + x.shape[1:])
        first, second = x[:, 0], x[:, 1]
        return jnp.concatenate(
            [jnp.where(y_hi == 0, first, second), jnp.where(y_hi == 0, second, first)], axis=0
        )

    def middle_grads(row_back, row_d_up):
        full_hidden = features_exchange(copies(hidden, parts))
        row_d_up = after(row_d_up, full_hidden)
        row_back = after(row_back, full_hidden[:few, :, :width])
        all_back = jnp.concatenate([row_back, swap_mates(row_back, 2)], axis=0)
        all_d_up = jnp.concatenate([row_d_up[:few], swap_mates(row_d_up[few:], 2)], axis=0)
        all_hidden = own_units(own_row_first(full_hidden))
        return weight_grads(both_cores(own_row_first(full_in)), all_hidden, all_back, all_d_up)

    def first_tick():
        return second_half(fresh, sums[block:], True)[:2] + (jnp.zeros(slope.shape, BF16),)

    down_mate = lax.cond(
        jnp.logical_and(segment > 0, segment < last),
        lambda: jnp.concatenate([down_other, swap_middle(down_other, 1)], axis=0),
        lambda: jnp.zeros_like(down_w),
    )

    up_mate_low = lax.cond(
        segment == last - 2,
        lambda: jnp.concatenate([up_other_low, swap_in_group(up_other_low, last - 2, 1)], axis=1),
        lambda: jnp.zeros_like(up_w),
    )

    def skip_first():
        moved = lax.ppermute(slope.astype(BF16), ("pipe", "dp", "tensor"), moves)
        return down_mate[:block] + up_mate_low[:block, :width], jnp.zeros((parts, block, 2 * units), BF16), moved

    out, full_d_up, middle_slope = lax.cond(segment == last, first_tick, skip_first)
    outs, kept_back, kept_d_up = [out], [], []
    for at in range(last - 1, 0, -1):
        if at == last - 1:
            row_back = rows_from_above(out, at)
            shape = row_back.shape
        else:
            row_back = row_sums_from_above(out, at)
            outs.append(lax.dynamic_index_in_dim(row_back, lax.axis_index("dp") // 4, 0, keepdims=False))
            shape = (block, width)
        out, row_d_up = lax.cond(
            segment == at,
            functools.partial(middle_tick, at),
            lambda row_back, shape=shape: (
                jnp.zeros(shape, BF16),
                jnp.zeros((parts, block, 2 * units), BF16),
            ),
            row_back,
        )
        kept_back.append(row_back)
        kept_d_up.append(row_d_up)
    outs.append(out)
    all_in, all_hidden = lax.cond(
        segment == 0,
        lambda: (both_cores(full_in), own_hidden()),
        lambda: (
            jnp.zeros((2 * chips, block, width), BF16),
            jnp.zeros((2 * parts, block, units), BF16),
        ),
    )
    received = lax.ppermute(out, "pipe", [(1, 0)])

    def end_lowest():
        out, full_back, full_d_up, part = tick(received)
        held = after(full_back[:1], part[:1])
        all_back = jnp.concatenate([held, full_back[1:], swap_cores(full_back)], axis=0)
        other = full_d_up[..., units:]
        first = jnp.concatenate([after(other[:1, :, :width], part[:1]), other[:1, :, width:]], axis=2)
        other = jnp.concatenate([first, other[1:]], axis=0)
        all_d_up = jnp.concatenate([full_d_up[..., :units], swap_cores(other)], axis=0)
        return (out,) + weight_products(all_in, all_hidden, all_back, all_d_up)

    def end_middle(k):
        return lambda: (outs[k + 1],) + middle_grads(kept_back[k], kept_d_up[k])

    def end_highest():
        return (outs[0],) + weight_grads(both_cores(full_in), own_hidden(), full_back, full_d_up)

    ends = [end_lowest] + [end_middle(last - 1 - at) for at in range(1, last)] + [end_highest]
    out, grad_up, grad_down = lax.switch(segment, ends)
    grads_in = jnp.swapaxes(out.reshape(rows, micro_count, width), 0, 1)
    return grads_in[None], grad_up[None], grad_down[None]


def solution(mesh):
    return jax.shard_map(
        body,
        mesh=mesh,
        in_specs=(
            P("pipe", None, "dp", "tensor"),
            P(None, "dp", "tensor"),
            P(),
            P("pipe", "tensor", "dp"),
            P("pipe", "dp", "tensor"),
        ),
        out_specs=(
            P("pipe", None, "dp", "tensor"),
            P("pipe", "tensor", "dp"),
            P("pipe", "dp", "tensor"),
        ),
        check_vma=False,
    )
```

```python
import functools

import jax
import jax.numpy as jnp
from jax import lax
from jax.sharding import PartitionSpec as P

BF16 = jnp.bfloat16
F32 = jnp.float32


def swap_cores(x):
    peers = lax.axis_size("dp")
    return lax.ppermute(x, "dp", [(i, i ^ 1) for i in range(peers)])


def chips_exchange(x):
    peers = lax.axis_size("dp")
    groups = [[i for i in range(peers) if i % 2 == core] for core in range(2)]
    return lax.all_to_all(x, "dp", 0, 0, axis_index_groups=groups, tiled=True)


def row_exchange(x):
    peers = lax.axis_size("dp")
    groups = [[4 * at + r for at in range(peers // 4)] for r in range(4)]
    return lax.all_to_all(x, "dp", 0, 0, axis_index_groups=groups, tiled=True)


def rows_from_above(x, at):
    segments, peers = lax.axis_size("pipe"), lax.axis_size("dp")
    few = peers // 4
    others = [p for p in range(segments) if p not in (at, at + 1)]
    groups = [
        [p * peers + 4 * k + r for p in two for k in range(few)]
        for two in ([at, at + 1], others)
        for r in range(4)
    ]
    x = lax.all_to_all(copies(x, 2 * few), ("pipe", "dp"), 0, 0, axis_index_groups=groups, tiled=True)
    return x[few:]


def row_sums_from_above(x, at):
    got = rows_from_above(x.reshape((-1,) + x.shape[2:]), at)
    return add_blocks(got).astype(BF16).reshape(x.shape)


def swap_middle(x, mate):
    segments, peers = lax.axis_size("pipe"), lax.axis_size("dp")
    pairs = [(p * peers + i, p * peers + (i ^ mate)) for p in range(1, segments - 1) for i in range(peers)]
    return lax.ppermute(x, ("pipe", "dp"), pairs)


def swap_in_group(x, group, mate):
    peers = lax.axis_size("dp")
    pairs = [(group * peers + i, group * peers + (i ^ mate)) for i in range(peers)]
    return lax.ppermute(x, ("pipe", "dp"), pairs)


def swap_mates(x, mate):
    return lax.ppermute(x, "dp", [(i, i ^ mate) for i in range(lax.axis_size("dp"))])


def features_exchange(x):
    return lax.all_to_all(x, "tensor", 0, 0, tiled=True)


def copies(x, count):
    return jnp.broadcast_to(x[None], (count,) + x.shape)


def add_blocks(x):
    return jnp.sum(x.astype(F32), axis=0)


def cols_product(left, right):
    return lax.dot_general(
        left, right, (((left.ndim - 1,), (1,)), ((), ())), preferred_element_type=F32
    )


def by_cols(left, right):
    return cols_product(left, right).astype(BF16)


def by_rows(left, right):
    dims = tuple(range(left.ndim - 1))
    return lax.dot_general(left, right, ((dims, dims), ((), ())), preferred_element_type=F32)


def body(saved, pool, picked, w_up, w_down):
    segments = lax.axis_size("pipe")
    segment = lax.axis_index("pipe")
    chips = lax.axis_size("dp") // 2
    parts = lax.axis_size("tensor")
    micro_count, rows, width = saved.shape[1:]
    units = w_up.shape[2]
    block = micro_count * rows
    last = segments - 1
    peers = lax.axis_size("dp")
    few = chips // 2
    y_hi = (lax.axis_index("dp") // 2) % 2

    up_w = jnp.concatenate([w_up[0], swap_cores(w_up[0])], axis=1)
    down_w = jnp.concatenate([w_down[0], swap_cores(w_down[0])], axis=0)

    up_other = swap_in_group(w_up[0], last - 1, 2)
    up_other_low = swap_in_group(w_up[0], last - 2, 2)
    down_other = swap_middle(w_down[0], 2)

    chosen = (picked[:, None] == jnp.arange(pool.shape[0])[None]).astype(BF16)
    fresh = jnp.einsum("ms,srd->rmd", chosen, pool, preferred_element_type=F32).astype(BF16)
    fresh = fresh.reshape(block, width)
    inputs = jnp.swapaxes(saved[0], 0, 1).reshape(block, width)

    gathered = chips_exchange(copies(jnp.concatenate([inputs, fresh], axis=0), chips))
    full_in = gathered[:, :block]
    full_back = gathered[:, block:]
    up_part = lax.dot_general(
        full_in, up_w, (((2,), (0,)), ((), ())), preferred_element_type=F32
    ).astype(BF16)
    back_part = by_cols(full_back, down_w)
    sums = add_blocks(features_exchange(jnp.concatenate([up_part, back_part], axis=1)))
    up = sums[:block]
    sig = jax.nn.sigmoid(up)
    hidden = (up * sig).astype(BF16)
    slope = sig * (1.0 + up * (1.0 - sig))

    moves = []
    for group in range(1, last):
        for i in range(peers):
            for z in range(parts):
                units_y, tokens_y = (i // 2) % 2, z % 2
                to = i - 2 * units_y + 2 * tokens_y
                place = (units_y ^ tokens_y) * few + z // 2
                moves.append(((group * peers + i) * parts + z, (group * peers + to) * parts + place))


    def after(x, y):
        return jnp.where(jnp.isnan(y), y, x)

    def second_half(arriving, back, stagger=False):
        d_up = (back * slope).astype(BF16)
        if stagger:
            pairs = [(last * peers + i, last * peers + (i ^ 4)) for i in range(0, peers, 2)]
            step = lax.ppermute(d_up, ("pipe", "dp"), pairs)
            d_up = after(d_up, step)
        full_d_up = features_exchange(copies(d_up, parts))
        part = by_cols(full_d_up, up_w)
        mixed = add_blocks(chips_exchange(part))
        return (arriving.astype(F32) + mixed).astype(BF16), full_d_up, part

    def both_cores(x):
        return jnp.concatenate([x, swap_cores(x)], axis=0)

    def own_units(x):
        return jnp.concatenate([x[..., :units], swap_cores(x[..., units:])], axis=0)

    def own_hidden():
        return own_units(features_exchange(copies(hidden, parts)))

    def weight_products(all_in, all_hidden, all_back, all_d_up):
        grad_up = by_rows(all_in, all_d_up).astype(BF16)
        grad_down = by_rows(all_hidden, all_back).astype(BF16)
        return grad_up, grad_down

    def weight_grads(all_in, all_hidden, full_back, full_d_up):
        return weight_products(all_in, all_hidden, both_cores(full_back), own_units(full_d_up))

    def one_step_later(x):
        return after(x, lax.ppermute(x, ("pipe", "dp"), [(i, i ^ 4) for i in range(1, peers, 2)]))

    def tick(arriving):
        sent = lax.cond(lax.axis_index("dp") % 2 == 1, one_step_later, lambda x: x, arriving)
        full_back = chips_exchange(copies(sent, chips))
        back = add_blocks(features_exchange(by_cols(full_back, down_w)))
        out, full_d_up, part = second_half(arriving, back)
        return out, full_back, full_d_up, part

    def middle_tick(at, row_back):
        row = lax.axis_index("dp") // 4
        if at == last - 1:
            up_mate = jnp.concatenate([up_other, swap_in_group(up_other, at, 1)], axis=1)
        else:
            up_mate = up_mate_low
        arriving = lax.dynamic_index_in_dim(row_back, row, 0, keepdims=False)
        part = jnp.concatenate([by_cols(row_back, down_w), by_cols(row_back, down_mate)], axis=0)
        back = add_blocks(features_exchange(part))
        d_up = (back * middle_slope).astype(BF16)
        row_d_up = features_exchange(copies(d_up, parts))
        part = cols_product(row_d_up[:few], up_w) + cols_product(row_d_up[few:], up_mate)
        if at == last - 1:
            mine = jnp.arange(few)[:, None, None] == row
            return (part + jnp.where(mine, row_back.astype(F32), 0.0)).astype(BF16), row_d_up
        mixed = add_blocks(row_exchange(part.astype(BF16)))
        return (arriving.astype(F32) + mixed).astype(BF16), row_d_up

    def own_row_first(x):
        x = x.reshape((few, 2) + x.shape[1:])
        first, second = x[:, 0], x[:, 1]
        return jnp.concatenate(
            [jnp.where(y_hi == 0, first, second), jnp.where(y_hi == 0, second, first)], axis=0
        )

    def middle_grads(row_back, row_d_up):
        full_hidden = features_exchange(copies(hidden, parts))
        row_d_up = after(row_d_up, full_hidden)
        row_back = after(row_back, full_hidden[:few, :, :width])
        all_back = jnp.concatenate([row_back, swap_mates(row_back, 2)], axis=0)
        all_d_up = jnp.concatenate([row_d_up[:few], swap_mates(row_d_up[few:], 2)], axis=0)
        all_hidden = own_units(own_row_first(full_hidden))
        return weight_grads(both_cores(own_row_first(full_in)), all_hidden, all_back, all_d_up)

    def first_tick():
        return second_half(fresh, sums[block:], True)[:2] + (jnp.zeros(slope.shape, BF16),)

    down_mate = lax.cond(
        jnp.logical_and(segment > 0, segment < last),
        lambda: jnp.concatenate([down_other, swap_middle(down_other, 1)], axis=0),
        lambda: jnp.zeros_like(down_w),
    )

    up_mate_low = lax.cond(
        segment == last - 2,
        lambda: jnp.concatenate([up_other_low, swap_in_group(up_other_low, last - 2, 1)], axis=1),
        lambda: jnp.zeros_like(up_w),
    )

    def skip_first():
        moved = lax.ppermute(slope.astype(BF16), ("pipe", "dp", "tensor"), moves)
        return down_mate[:block] + up_mate_low[:block, :width], jnp.zeros((parts, block, 2 * units), BF16), moved

    out, full_d_up, middle_slope = lax.cond(segment == last, first_tick, skip_first)
    outs, kept_back, kept_d_up = [out], [], []
    for at in range(last - 1, 0, -1):
        if at == last - 1:
            row_back = rows_from_above(out, at)
            shape = row_back.shape
        else:
            row_back = row_sums_from_above(out, at)
            outs.append(lax.dynamic_index_in_dim(row_back, lax.axis_index("dp") // 4, 0, keepdims=False))
            shape = (block, width)
        out, row_d_up = lax.cond(
            segment == at,
            functools.partial(middle_tick, at),
            lambda row_back, shape=shape: (
                jnp.zeros(shape, BF16),
                jnp.zeros((parts, block, 2 * units), BF16),
            ),
            row_back,
        )
        kept_back.append(row_back)
        kept_d_up.append(row_d_up)
    outs.append(out)
    all_in, all_hidden = lax.cond(
        segment == 0,
        lambda: (both_cores(full_in), own_hidden()),
        lambda: (
            jnp.zeros((2 * chips, block, width), BF16),
            jnp.zeros((2 * parts, block, units), BF16),
        ),
    )
    received = lax.ppermute(out, "pipe", [(1, 0)])

    def end_lowest():
        out, full_back, full_d_up, part = tick(received)
        held = after(full_back[:1], part[:1])
        all_back = jnp.concatenate([held, full_back[1:], swap_cores(full_back)], axis=0)
        other = full_d_up[..., units:]
        first = jnp.concatenate([after(other[:1, :, :width], part[:1]), other[:1, :, width:]], axis=2)
        other = jnp.concatenate([first, other[1:]], axis=0)
        all_d_up = jnp.concatenate([full_d_up[..., :units], swap_cores(other)], axis=0)
        return (out,) + weight_products(all_in, all_hidden, all_back, all_d_up)

    def end_middle(k):
        return lambda: (outs[k + 1],) + middle_grads(kept_back[k], kept_d_up[k])

    def end_highest():
        return (outs[0],) + weight_grads(both_cores(full_in), own_hidden(), full_back, full_d_up)

    ends = [end_lowest] + [end_middle(last - 1 - at) for at in range(1, last)] + [end_highest]
    out, grad_up, grad_down = lax.switch(segment, ends)
    grads_in = jnp.swapaxes(out.reshape(rows, micro_count, width), 0, 1)
    return grads_in[None], grad_up[None], grad_down[None]


def solution(mesh):
    return jax.shard_map(
        body,
        mesh=mesh,
        in_specs=(
            P("pipe", None, "dp", "tensor"),
            P(None, "dp", "tensor"),
            P(),
            P("pipe", "tensor", "dp"),
            P("pipe", "dp", "tensor"),
        ),
        out_specs=(
            P("pipe", None, "dp", "tensor"),
            P("pipe", "tensor", "dp"),
            P("pipe", "dp", "tensor"),
        ),
        check_vma=False,
    )
```
